512 devices in a mesh: chan: 4 (over y), row: 16 (over x, z_hi), col: 8 (over z_lo, core).
Axes of the slice: x: 4, y: 4, z: 16 (z_hi: 4, z_lo: 4; z = z_hi * 4 + z_lo), core: 2. Of those that a mesh axis runs over, the one named last changes fastest.
Arguments:
- voltages: bfloat16 [32, 2, 4096, 256], P('chan', None, ('row', 'col')), parts along dimension 0
- model: bfloat16 [32, 2, 4096, 4096], P('chan', None, 'row', 'col'), parts along dimension 0, as said below
Outputs:
- gains: float32 [32, 2, 4096], P('chan', None, 'col'), parts along dimension 0
- misfit: float32 [32, 4096], P('chan', 'col'), parts along dimension 0
There are 4 independent parts, one for each index of `chan`. The reference program is written for one: setup_inputs(seed, part) draws one part's arguments, and reference() takes and returns one part's arrays. A program takes and returns all parts, laid end to end along the dimension named above; each array names one. Nothing has to cross between parts.
Inputs may be any that keep to these rules, and one draw needn't show every extreme that they name: In every channel the model matrix is Hermitian: its real part is symmetric and its imaginary part antisymmetric.
All inputs are finite; a program needn't handle non-finite values.
Results may differ from the reference program's by a relative error of at most 0.0003.
Values may be sent and summed in bfloat16 or wider, within the bound.
A program may use at most 192 MiB of HBM per device.

```python
import math
import jax
import jax.numpy as jnp
from jax import lax

CH = 8
TIME = 256
ITERS = 3
INPUTS = 4096


MODEL_SCALE = 0.125


MODEL_ERROR = 0.75


def sky_terms(key, flux_low, flux_high):
    keys = jax.random.split(key, 4)
    phases = jax.random.uniform(keys[0], (CH, INPUTS, 8), jnp.float32, -math.pi, math.pi)
    fluxes = jnp.exp(jax.random.uniform(keys[1], (CH, 8), jnp.float32, math.log(flux_low), math.log(flux_high)))
    position = jnp.arange(INPUTS, dtype=jnp.float32) / INPUTS
    amplitude = 0.4 * jnp.exp(position * math.log(6.0))[None, :] * jnp.exp(jax.random.uniform(keys[2], (CH, INPUTS), jnp.float32, -0.2, 0.2))
    gain_phase = jax.random.uniform(keys[3], (CH, INPUTS), jnp.float32, -1.0, 1.0)
    return (phases, fluxes, amplitude, gain_phase)


def draw_voltages(key, part):
    phases, fluxes, amplitude, gain_phase = sky_terms(key, 0.02, 0.2)
    key = jax.random.fold_in(key, 5)
    keys = jax.random.split(key, 4)
    signal_re = jnp.clip(jax.random.normal(keys[0], (CH, 8, TIME), jnp.float32), -4.0, 4.0) * math.sqrt(0.5)
    signal_im = jnp.clip(jax.random.normal(keys[1], (CH, 8, TIME), jnp.float32), -4.0, 4.0) * math.sqrt(0.5)
    noise_re = jnp.clip(jax.random.normal(keys[2], (CH, INPUTS, TIME), jnp.float32), -4.0, 4.0) * math.sqrt(0.5)
    noise_im = jnp.clip(jax.random.normal(keys[3], (CH, INPUTS, TIME), jnp.float32), -4.0, 4.0) * math.sqrt(0.5)
    field_re = jnp.zeros((CH, INPUTS, TIME), jnp.float32)
    field_im = jnp.zeros((CH, INPUTS, TIME), jnp.float32)
    for source in range(8):
        weight = jnp.sqrt(fluxes[:, source])[:, None, None]
        cosine = jnp.cos(phases[:, :, source])[:, :, None]
        sine = jnp.sin(phases[:, :, source])[:, :, None]
        wave_re = signal_re[:, source][:, None, :]
        wave_im = signal_im[:, source][:, None, :]
        field_re = field_re + weight * (cosine * wave_re - sine * wave_im)
        field_im = field_im + weight * (cosine * wave_im + sine * wave_re)
    turn_re = (amplitude * jnp.cos(gain_phase))[:, :, None]
    turn_im = (amplitude * jnp.sin(gain_phase))[:, :, None]
    volt_re = turn_re * field_re - turn_im * field_im + noise_re
    volt_im = turn_re * field_im + turn_im * field_re + noise_im
    return jnp.stack([volt_re, volt_im], axis=1).astype(jnp.bfloat16)


def draw_model(key, part):
    phases, fluxes, amplitude, gain_phase = sky_terms(key, 0.02, 0.2)
    key = jax.random.fold_in(key, 7)

    def channel_model(arguments):
        channel, phase_table, flux_table = arguments
        model_re = jnp.zeros((INPUTS, INPUTS), jnp.float32)
        model_im = jnp.zeros((INPUTS, INPUTS), jnp.float32)
        for source in range(8):
            differ = phase_table[:, source][:, None] - phase_table[:, source][None, :]
            model_re = model_re + flux_table[source] * jnp.cos(differ)
            model_im = model_im + flux_table[source] * jnp.sin(differ)
        errors = jax.random.normal(jax.random.fold_in(key, channel), (2, INPUTS, INPUTS), jnp.float32) * MODEL_ERROR
        model_re = model_re + (errors[0] + errors[0].T) * 0.5
        model_im = model_im + (errors[1] - errors[1].T) * 0.5
        return jnp.stack([model_re, model_im]) * MODEL_SCALE
    return lax.map(channel_model, (jnp.arange(CH, dtype=jnp.int32), phases, fluxes)).astype(jnp.bfloat16)


def setup_inputs(seed: int = 0, part: int = 0) -> dict:
    key_list = jax.random.split(jax.random.key(seed), 3)
    part_keys = jax.random.split(jax.random.fold_in(key_list[2], part), 3)
    return {
        "voltages": draw_voltages(jax.random.fold_in(jax.random.fold_in(key_list[2], part), 71), part),
        "model": draw_model(jax.random.fold_in(jax.random.fold_in(key_list[2], part), 71), part),
    }


EPSILON = 1e-6


def gram_parts(voltage_block):
    real_part = voltage_block[0].astype(jnp.float32)
    imag_part = voltage_block[1].astype(jnp.float32)
    highest = lax.Precision.HIGHEST
    vis_real = (jnp.dot(real_part, real_part.T, precision=highest) + jnp.dot(imag_part, imag_part.T, precision=highest)) * (1.0 / TIME)
    vis_imag = (jnp.dot(imag_part, real_part.T, precision=highest) - jnp.dot(real_part, imag_part.T, precision=highest)) * (1.0 / TIME)
    return vis_real, vis_imag


def calibrate(arguments):
    voltage_block, model_block = arguments
    vis_real, vis_imag = gram_parts(voltage_block)
    mod_real = model_block[0].astype(jnp.float32)
    mod_imag = model_block[1].astype(jnp.float32)
    off_diag = 1.0 - jnp.eye(INPUTS, dtype=jnp.float32)
    gain_real = jnp.ones((INPUTS,), jnp.float32)
    gain_imag = jnp.zeros((INPUTS,), jnp.float32)
    for iteration in range(ITERS):
        along_re = gain_real[:, None] * mod_real - gain_imag[:, None] * mod_imag
        along_im = gain_real[:, None] * mod_imag + gain_imag[:, None] * mod_real
        numer_re = jnp.sum(off_diag * (vis_real * along_re + vis_imag * along_im), axis=0)
        numer_im = jnp.sum(off_diag * (vis_real * along_im - vis_imag * along_re), axis=0)
        denom = jnp.sum(off_diag * (along_re * along_re + along_im * along_im), axis=0) + EPSILON
        fresh_re = numer_re / denom
        fresh_im = numer_im / denom
        if iteration % 2 == 1:
            fresh_re = (fresh_re + gain_real) * 0.5
            fresh_im = (fresh_im + gain_imag) * 0.5
        gain_real = fresh_re
        gain_imag = fresh_im
    along_re = gain_real[:, None] * mod_real - gain_imag[:, None] * mod_imag
    along_im = gain_real[:, None] * mod_imag + gain_imag[:, None] * mod_real
    error_re = vis_real - (along_re * gain_real[None, :] + along_im * gain_imag[None, :])
    error_im = vis_imag - (along_im * gain_real[None, :] - along_re * gain_imag[None, :])
    misfit = jnp.sum(off_diag * (error_re * error_re + error_im * error_im), axis=0) / (INPUTS - 1)
    return jnp.stack([gain_real, gain_imag]), misfit


def reference(voltages, model):
    gains, misfit = lax.map(calibrate, (voltages, model))
    return gains, misfit
```

```python
import functools

import jax
import jax.numpy as jnp
from jax import lax
from jax.experimental import pallas as pl
from jax.experimental.pallas import tpu as pltpu
from jax.sharding import PartitionSpec as P

EPSILON = 1e-06
MESH = pl.DeviceIdType.MESH
F32 = jnp.float32

RING = 16
SEG = 4
XS = 4
LINE = 2 * RING
HALF = RING
CHUNKS = 2
STEPS = (RING // 2 + 1) * CHUNKS
ROWS = 16
TILE = (8, 128)


def div(a, b):
    return lax.div(a, jnp.int32(b))


def rem(a, b):
    return lax.rem(a, jnp.int32(b))


def kernel(
    volts, model, gains_out, misfit_out,
    buf, mod, vis, spread, sbuf, rbuf, total, gtile, gbuf, cbuf, mtile, mbuf,
    load_sem, ring_send, ring_recv, sib_send, sib_recv, chain_send, chain_recv,
    part_send, part_recv, gain_send, gain_recv, col_send, col_recv, mis_send, mis_recv,
):
    channels = mod.shape[0]
    samples = volts.shape[3]
    per_chunk = channels // CHUNKS
    inputs = 4096
    r = lax.axis_index("row")
    c = lax.axis_index("col")
    x, zh = div(r, SEG), rem(r, SEG)
    zl, k = div(c, 2), rem(c, 2)
    z = zh * SEG + zl
    hub = x == zl
    odd = rem(r, 2)
    own_row = div(r, 2) == c

    def place(xx, zz, kk):
        return {"row": xx * SEG + div(zz, SEG), "col": rem(zz, SEG) * 2 + kk}

    own_slot = z * 2 + k
    load_volts = pltpu.make_async_copy(volts, buf.at[own_slot], load_sem.at[0])
    load_model = pltpu.make_async_copy(model, mod, load_sem.at[1])
    load_volts.start()
    load_model.start()

    barrier = pltpu.get_barrier_semaphore()

    def signal(target):
        pl.semaphore_signal(barrier, inc=1, device_id=target, device_id_type=MESH)

    signal(place(x, rem(z + 1, RING), k))
    signal(place(x, rem(z + RING - 1, RING), k))
    signal(place(x, z, 1 - k))

    def greet(i, _):
        @pl.when(i != r)
        def _():
            signal({"row": i, "col": c})
        return 0

    lax.fori_loop(0, 2 * channels, greet, 0)

    def greet_owner(ch, _):
        @pl.when(jnp.logical_not(jnp.logical_and(own_row, ch == c)))
        def _():
            signal({"row": 2 * ch + odd, "col": div(r, 2)})
        return 0

    lax.fori_loop(0, channels, greet_owner, 0)
    sbuf[...] = jnp.zeros(sbuf.shape, F32)
    gtile[...] = jnp.zeros(gtile.shape, F32)
    mtile[...] = jnp.zeros(mtile.shape, F32)
    load_volts.wait()
    pl.semaphore_wait(barrier, 3 + 2 * channels - 1 + channels - own_row.astype(jnp.int32))

    def chunk(slot, q):
        return buf.at[slot, pl.ds(q * per_chunk, per_chunk)]

    def reach(way, q):
        return RING // 2 - rem(q + way, 2)

    def shard(way, t):
        return rem(z - t + RING, RING) if way == 0 else rem(z + t, RING)

    def exists(way, t, q):
        here = t <= reach(way, q)
        return here if way == 0 else jnp.logical_and(here, t >= 1)

    def ring_copy(way, n):
        t, q = div(n, CHUNKS), rem(n, CHUNKS)
        slot = shard(way, t) * 2 + k
        nxt = rem(z + 1, RING) if way == 0 else rem(z + RING - 1, RING)
        return pltpu.make_async_remote_copy(
            src_ref=chunk(slot, q), dst_ref=chunk(slot, q),
            send_sem=ring_send.at[way, n], recv_sem=ring_recv.at[way, n + CHUNKS],
            device_id=place(x, nxt, k), device_id_type=MESH)

    def arrival(slot, q, sem):
        return pltpu.make_async_copy(chunk(slot, q), chunk(slot, q), sem)

    def sib_copy(way, n):
        t, q = div(n, CHUNKS), rem(n, CHUNKS)
        slot = shard(way, t) * 2 + k
        return pltpu.make_async_remote_copy(
            src_ref=chunk(slot, q), dst_ref=chunk(slot, q),
            send_sem=sib_send.at[way, n], recv_sem=sib_recv.at[way, n],
            device_id=place(x, z, 1 - k), device_id_type=MESH)

    def sib_wanted(way, n, core):
        t, q = div(n, CHUNKS), rem(n, CHUNKS)
        zz = shard(way, t)
        use = jnp.logical_or(
            div(zz, SEG) == zh, jnp.logical_and(hub, div(zz, RING // 2) == core))
        return jnp.logical_and(exists(way, t, q), use)

    def chain_place(core):
        if core == 0:
            return rem(x - zl + XS, XS), rem(x + 1, XS)
        return rem(zl - x + XS, XS), rem(x + XS - 1, XS)

    def chain_copy(core, way, m):
        t, q = div(m, CHUNKS), rem(m, CHUNKS)
        zz = shard(way, t)
        _, nxt = chain_place(core)
        to = LINE + rem(zz, RING // 2) * 2 + core
        slot = jnp.where(hub, zz * 2 + core, to)
        return pltpu.make_async_remote_copy(
            src_ref=chunk(slot, q), dst_ref=chunk(to, q),
            send_sem=chain_send.at[core, way, m], recv_sem=chain_recv.at[core, way, m],
            device_id=place(nxt, z, k), device_id_type=MESH)

    def chain_wanted(way, m):
        t, q = div(m, CHUNKS), rem(m, CHUNKS)
        mine = div(shard(way, t), RING // 2) == k
        inside = jnp.logical_and(m >= 0, m < STEPS)
        return jnp.logical_and(inside, jnp.logical_and(exists(way, t, q), mine))

    def gather(n, _):
        t, q = div(n, CHUNKS), rem(n, CHUNKS)
        for way in (0, 1):
            @pl.when(jnp.logical_and(n < STEPS, t <= reach(way, q)))
            def _():
                @pl.when(t >= 1)
                def _():
                    arrival(shard(way, t) * 2 + k, q, ring_recv.at[way, n]).wait()

                @pl.when(t < reach(way, q))
                def _():
                    ring_copy(way, n).start()

                @pl.when(sib_wanted(way, n, 1 - k))
                def _():
                    sib_copy(way, n).start()
        m = jnp.maximum(n - 1, 0)
        for way in (0, 1):
            @pl.when(jnp.logical_and(jnp.logical_and(n >= 1, n <= STEPS), sib_wanted(way, m, k)))
            def _():
                arrival(shard(way, div(m, CHUNKS)) * 2 + 1 - k, rem(m, CHUNKS), sib_recv.at[way, m]).wait()
        for core in (0, 1):
            far, _ = chain_place(core)
            raw = n - 1 - far
            m = jnp.maximum(raw, 0)
            for way in (0, 1):
                @pl.when(jnp.logical_and(raw >= 0, chain_wanted(way, m)))
                def _():
                    @pl.when(far >= 1)
                    def _():
                        zz = shard(way, div(m, CHUNKS))
                        slot = LINE + rem(zz, RING // 2) * 2 + core
                        arrival(slot, rem(m, CHUNKS), chain_recv.at[core, way, m]).wait()

                    @pl.when(far < XS - 1)
                    def _():
                        chain_copy(core, way, m).start()
        return 0

    lax.fori_loop(0, STEPS + XS, gather, 0)

    def settle(n, _):
        t, q = div(n, CHUNKS), rem(n, CHUNKS)
        for way in (0, 1):
            @pl.when(t < reach(way, q))
            def _():
                ring_copy(way, n).wait_send()

            @pl.when(sib_wanted(way, n, 1 - k))
            def _():
                sib_copy(way, n).wait_send()

            for core in (0, 1):
                far, _ = chain_place(core)

                @pl.when(jnp.logical_and(far < XS - 1, chain_wanted(way, n)))
                def _():
                    chain_copy(core, way, n).wait_send()
        return 0

    width = vis.shape[3]
    height = vis.shape[2]
    half = width // 2
    lanes = TILE[1]
    row_base = zh * (2 * SEG)
    col_base = jnp.where(hub, k * HALF, LINE)
    load_model.wait()

    def part_copy(phase, target):
        return pltpu.make_async_remote_copy(
            src_ref=sbuf.at[phase, target], dst_ref=rbuf.at[phase, r],
            send_sem=part_send.at[phase], recv_sem=part_recv.at[phase],
            device_id={"row": target, "col": c}, device_id_type=MESH)

    def hand_in(phase, target):
        @pl.when(target != r)
        def _():
            part_copy(phase, target).start()

        @pl.when(target == r)
        def _():
            rbuf[phase, r] = sbuf[phase, r]

    def put(phase, target, first, value):
        for j in range(half // lanes):
            sbuf[phase, target, first + j : first + j + 1, :] = value[:, j * lanes : (j + 1) * lanes]

    def fold(value):
        return jnp.sum(value.reshape(ROWS // 8, 8, half), axis=0)

    def wide(value):
        return jnp.concatenate([value] * (half // lanes), axis=1)

    def along(ch, rows, cols, plain):
        mr = mod[ch, 0, rows, cols].astype(F32)
        mi = mod[ch, 1, rows, cols].astype(F32)
        if plain:
            return mr, mi
        gr = wide(spread[ch, 0, rows, :])
        gi = wide(spread[ch, 1, rows, :])
        return gr * mr - gi * mi, gr * mi + gi * mr

    def normal_sums(phase, ch):
        for b in (0, 1):
            cols = slice(b * half, (b + 1) * half)

            def body(i, acc):
                rows = pl.ds(pl.multiple_of(i * ROWS, ROWS), ROWS)
                vr = vis[ch, 0, rows, cols]
                vi = vis[ch, 1, rows, cols]
                ar, ai = along(ch, rows, cols, phase == 0)
                return (
                    acc[0] + fold(vr * ar + vi * ai),
                    acc[1] + fold(vr * ai - vi * ar),
                    acc[2] + fold(ar * ar + ai * ai),
                )

            zero = jnp.zeros((8, half), F32)
            sums = lax.fori_loop(0, height // ROWS, body, (zero, zero, zero), unroll=4)
            for i, value in enumerate(sums):
                put(phase, 2 * ch + b, 2 * i, jnp.sum(value, axis=0, keepdims=True))
            hand_in(phase, 2 * ch + b)

    def misfit_sums(phase, ch):
        for b in (0, 1):
            cols = slice(b * half, (b + 1) * half)
            cr = jnp.concatenate([cbuf[2 * ch + b, 0:1, :], cbuf[2 * ch + b, 1:2, :]], axis=1)
            ci = jnp.concatenate([cbuf[2 * ch + b, 2:3, :], cbuf[2 * ch + b, 3:4, :]], axis=1)

            def body(i, acc):
                rows = pl.ds(pl.multiple_of(i * ROWS, ROWS), ROWS)
                ar, ai = along(ch, rows, cols, False)
                er = vis[ch, 0, rows, cols] - (ar * cr + ai * ci)
                ei = vis[ch, 1, rows, cols] - (ai * cr - ar * ci)
                return acc + fold(er * er + ei * ei)

            total_here = lax.fori_loop(0, height // ROWS, body, jnp.zeros((8, half), F32), unroll=4)
            put(phase, 2 * ch + b, 0, jnp.sum(total_here, axis=0, keepdims=True))
            hand_in(phase, 2 * ch + b)

    def no_diagonal(ref, ch):
        for b in (0, 1):
            @pl.when(jnp.logical_and(own_row, odd == b))
            def _():
                for comp in (0, 1):
                    def body(i, _):
                        for j in range(half // lanes):
                            rows = pl.ds(pl.multiple_of(j * lanes + i * ROWS, ROWS), ROWS)
                            cols = slice(b * half + j * lanes, b * half + (j + 1) * lanes)
                            row_id = lax.broadcasted_iota(jnp.int32, (ROWS, lanes), 0) + i * ROWS
                            col_id = lax.broadcasted_iota(jnp.int32, (ROWS, lanes), 1)
                            tile = ref[ch, comp, rows, cols].astype(F32)
                            ref[ch, comp, rows, cols] = jnp.where(row_id == col_id, 0.0, tile).astype(ref.dtype)
                        return 0

                    lax.fori_loop(0, lanes // ROWS, body, 0)

    def first(ch, _):
        row_re = buf[pl.ds(row_base, 2 * SEG), ch, 0].reshape(height, samples)
        row_im = buf[pl.ds(row_base, 2 * SEG), ch, 1].reshape(height, samples)
        col_re = buf[pl.ds(col_base, HALF), ch, 0].reshape(width, samples)
        col_im = buf[pl.ds(col_base, HALF), ch, 1].reshape(width, samples)

        def gram(a, b):
            return lax.dot_general(a, b, (((1,), (1,)), ((), ())), preferred_element_type=F32)

        vis[ch, 0] = (gram(row_re, col_re) + gram(row_im, col_im)) * (1.0 / samples)
        vis[ch, 1] = (gram(row_im, col_re) - gram(row_re, col_im)) * (1.0 / samples)
        no_diagonal(vis, ch)
        no_diagonal(mod, ch)
        normal_sums(0, ch)
        return 0

    def collect(phase):
        part = rbuf.at[phase, pl.ds(0, 2 * channels - 1)]
        pltpu.make_async_copy(part, part, part_recv.at[phase]).wait()
        total[...] = jnp.sum(rbuf[phase], axis=0)

    def gain_copy(phase, i):
        return pltpu.make_async_remote_copy(
            src_ref=gtile.at[phase], dst_ref=gbuf.at[phase, div(r, 2)],
            send_sem=gain_send.at[phase], recv_sem=gain_recv.at[phase, div(r, 2)],
            device_id={"row": 2 * c + odd, "col": i}, device_id_type=MESH)

    def col_copy(tile, dst, send, recv, i):
        return pltpu.make_async_remote_copy(
            src_ref=tile, dst_ref=dst.at[r], send_sem=send, recv_sem=recv,
            device_id={"row": i, "col": c}, device_id_type=MESH)

    def to_column(tile, dst, send, recv):
        def body(i, _):
            @pl.when(i != r)
            def _():
                col_copy(tile, dst, send, recv, i).start()
            return 0

        lax.fori_loop(0, 2 * channels, body, 0)
        dst[r] = tile[...]

    def wait_column(dst, sem):
        part = dst.at[pl.ds(0, 2 * channels - 1)]
        pltpu.make_async_copy(part, part, sem).wait()

    def own_gains(phase):
        collect(phase)
        den = total[4:6, :] + EPSILON
        fresh_re = total[0:2, :] / den
        fresh_im = total[2:4, :] / den
        if phase % 2 == 1:
            fresh_re = (fresh_re + gtile[phase - 1, 0:2, :]) * 0.5
            fresh_im = (fresh_im + gtile[phase - 1, 2:4, :]) * 0.5
        gtile[phase, 0:2, :] = fresh_re
        gtile[phase, 2:4, :] = fresh_im

        def body(i, _):
            @pl.when(jnp.logical_not(jnp.logical_and(own_row, i == c)))
            def _():
                gain_copy(phase, i).start()
            return 0

        lax.fori_loop(0, channels, body, 0)

        @pl.when(own_row)
        def _():
            gbuf[phase, div(r, 2)] = gtile[phase]

    def take_gains(phase, ch):
        @pl.when(jnp.logical_not(jnp.logical_and(own_row, ch == c)))
        def _():
            part = gbuf.at[phase, ch]
            pltpu.make_async_copy(part, part, gain_recv.at[phase, ch]).wait()
        for comp in (0, 1):
            for j in range(height // lanes):
                line = gbuf[phase, ch, 2 * comp + j : 2 * comp + j + 1, :]
                spread[ch, comp, j * lanes : (j + 1) * lanes, :] = jnp.broadcast_to(line, (lanes, lanes)).T

    lax.fori_loop(0, channels, first, 0)
    own_gains(0)
    for phase in (1, 2):
        def again(ch, _):
            take_gains(phase - 1, ch)
            normal_sums(phase, ch)
            return 0

        lax.fori_loop(0, channels, again, 0)
        own_gains(phase)
    to_column(gtile.at[2], cbuf, col_send, col_recv)

    def last(ch, _):
        take_gains(2, ch)
        misfit_sums(3, ch)
        return 0

    wait_column(cbuf, col_recv)
    lax.fori_loop(0, channels, last, 0)
    collect(3)
    mtile[0:2, :] = total[0:2, :] / (inputs - 1)
    to_column(mtile, mbuf, mis_send, mis_recv)
    for ch in range(channels):
        for b in (0, 1):
            for j in range(half // lanes):
                cols = slice(b * half + j * lanes, b * half + (j + 1) * lanes)
                for comp in (0, 1):
                    gains_out[ch, comp : comp + 1, cols] = cbuf[2 * ch + b, 2 * comp + j : 2 * comp + j + 1, :]

    lax.fori_loop(0, STEPS, settle, 0)
    for phase in range(4):
        part = sbuf.at[phase, pl.ds(0, 2 * channels - 1)]
        pltpu.make_async_copy(part, part, part_send.at[phase]).wait()
    for phase in range(3):
        for sent, there in ((channels - 1, own_row), (channels, jnp.logical_not(own_row))):
            @pl.when(there)
            def _():
                part = gbuf.at[phase, pl.ds(0, sent)]
                pltpu.make_async_copy(part, part, gain_send.at[phase]).wait()
    wait_column(cbuf, col_send)
    wait_column(mbuf, mis_send)
    wait_column(mbuf, mis_recv)
    for ch in range(channels):
        for b in (0, 1):
            for j in range(half // lanes):
                cols = slice(b * half + j * lanes, b * half + (j + 1) * lanes)
                misfit_out[ch : ch + 1, cols] = mbuf[2 * ch + b, j : j + 1, :]


def per_device(voltages, model):
    channels, _, shard_rows, samples = voltages.shape
    height, width = model.shape[2:]
    dma = pltpu.SemaphoreType.DMA
    return pl.pallas_call(
        kernel,
        out_shape=(
            jax.ShapeDtypeStruct((channels, 2, width), F32),
            jax.ShapeDtypeStruct((channels, width), F32),
        ),
        in_specs=[pl.BlockSpec(memory_space=pl.ANY)] * 2,
        out_specs=(pl.BlockSpec(memory_space=pltpu.VMEM),) * 2,
        scratch_shapes=[
            pltpu.VMEM((LINE + HALF,) + voltages.shape, voltages.dtype),
            pltpu.VMEM(model.shape, model.dtype),
            pltpu.VMEM((channels, 2, height, width), F32),
            pltpu.VMEM((channels, 2, height, TILE[1]), F32),
            pltpu.VMEM((4, 2 * channels) + TILE, F32),
            pltpu.VMEM((4, 2 * channels) + TILE, F32),
            pltpu.VMEM(TILE, F32),
            pltpu.VMEM((3,) + TILE, F32),
            pltpu.VMEM((3, channels) + TILE, F32),
            pltpu.VMEM((2 * channels,) + TILE, F32),
            pltpu.VMEM(TILE, F32),
            pltpu.VMEM((2 * channels,) + TILE, F32),
            dma((2,)),
            dma((2, STEPS)),
            dma((2, STEPS)),
            dma((2, STEPS)),
            dma((2, STEPS)),
            dma((2, 2, STEPS)),
            dma((2, 2, STEPS)),
            dma((4,)),
            dma((4,)),
            dma((3,)),
            dma((3, channels)),
            dma(()),
            dma(()),
            dma(()),
            dma(()),
        ],
        compiler_params=pltpu.CompilerParams(
            collective_id=0, has_side_effects=True, vmem_limit_bytes=50 * 2**20
        ),
    )(voltages, model)


def solution(mesh):
    return jax.shard_map(
        per_device,
        mesh=mesh,
        in_specs=(P("chan", None, ("row", "col"), None), P("chan", None, "row", "col")),
        out_specs=(P("chan", None, "col"), P("chan", "col")),
        check_vma=False,
    )
```

```python
import functools

import jax
import jax.numpy as jnp
from jax import lax
from jax.experimental import pallas as pl
from jax.experimental.pallas import tpu as pltpu
from jax.sharding import PartitionSpec as P

EPSILON = 1e-06
MESH = pl.DeviceIdType.MESH
F32 = jnp.float32

RING = 16
SEG = 4
XS = 4
LINE = 2 * RING
HALF = RING
GROUPS = 2
SUBS = 2
SPAN = (RING // 2 + 1) * SUBS
STEPS = GROUPS * SPAN
LAG = 2
ROWS = 32
TILE = (8, 128)


def div(a, b):
    return lax.div(a, jnp.int32(b))


def rem(a, b):
    return lax.rem(a, jnp.int32(b))


def kernel(
    volts, model, gains_out, misfit_out,
    buf, mod, vis, spread, sbuf, rbuf, total, gtile, gbuf, cbuf, mtile, mbuf,
    load_sem, ring_send, ring_recv, sib_send, sib_recv, chain_send, chain_recv,
    part_send, part_recv, gain_send, gain_recv, col_send, col_recv, mis_send, mis_recv,
):
    channels = mod.shape[0]
    samples = volts.shape[3]
    per_chunk = channels // (GROUPS * SUBS)
    per_group = channels // GROUPS
    inputs = 4096
    r = lax.axis_index("row")
    c = lax.axis_index("col")
    x, zh = div(r, SEG), rem(r, SEG)
    zl, k = div(c, 2), rem(c, 2)
    z = zh * SEG + zl
    hub = x == zl
    odd = rem(r, 2)
    own_group = div(r, 2 * per_group)
    own_row = div(r, 2) == c

    def place(xx, zz, kk):
        return {"row": xx * SEG + div(zz, SEG), "col": rem(zz, SEG) * 2 + kk}

    own_slot = z * 2 + k
    load_volts = pltpu.make_async_copy(volts, buf.at[own_slot], load_sem.at[0])
    load_model = pltpu.make_async_copy(model, mod, load_sem.at[1])
    load_volts.start()
    load_model.start()

    barrier = pltpu.get_barrier_semaphore()

    def signal(target):
        pl.semaphore_signal(barrier, inc=1, device_id=target, device_id_type=MESH)

    signal(place(x, rem(z + 1, RING), k))
    signal(place(x, rem(z + RING - 1, RING), k))
    signal(place(x, z, 1 - k))

    def greet(i, _):
        @pl.when(i != r)
        def _():
            signal({"row": i, "col": c})
        return 0

    lax.fori_loop(0, 2 * channels, greet, 0)

    def greet_owner(ch, _):
        @pl.when(jnp.logical_not(jnp.logical_and(own_row, ch == c)))
        def _():
            signal({"row": 2 * ch + odd, "col": div(r, 2)})
        return 0

    lax.fori_loop(0, channels, greet_owner, 0)
    sbuf[...] = jnp.zeros(sbuf.shape, F32)
    gtile[...] = jnp.zeros(gtile.shape, F32)
    mtile[...] = jnp.zeros(mtile.shape, F32)
    load_volts.wait()
    pl.semaphore_wait(barrier, 3 + 2 * channels - 1 + channels - own_row.astype(jnp.int32))

    def split(n):
        sub = rem(n, SUBS)
        return div(rem(n, SPAN), SUBS), sub, div(n, SPAN) * SUBS + sub

    def chunk(slot, q):
        return buf.at[slot, pl.ds(q * per_chunk, per_chunk)]

    def reach(way, sub):
        return RING // 2 - rem(sub + way, 2)

    def shard(way, t):
        return rem(z - t + RING, RING) if way == 0 else rem(z + t, RING)

    def exists(way, t, sub):
        here = t <= reach(way, sub)
        return here if way == 0 else jnp.logical_and(here, t >= 1)

    def ring_copy(way, n):
        t, sub, q = split(n)
        slot = shard(way, t) * 2 + k
        nxt = rem(z + 1, RING) if way == 0 else rem(z + RING - 1, RING)
        return pltpu.make_async_remote_copy(
            src_ref=chunk(slot, q), dst_ref=chunk(slot, q),
            send_sem=ring_send.at[way, n], recv_sem=ring_recv.at[way, n + SUBS],
            device_id=place(x, nxt, k), device_id_type=MESH)

    def arrival(slot, q, sem):
        return pltpu.make_async_copy(chunk(slot, q), chunk(slot, q), sem)

    def sib_copy(way, n):
        t, sub, q = split(n)
        slot = shard(way, t) * 2 + k
        return pltpu.make_async_remote_copy(
            src_ref=chunk(slot, q), dst_ref=chunk(slot, q),
            send_sem=sib_send.at[way, n], recv_sem=sib_recv.at[way, n],
            device_id=place(x, z, 1 - k), device_id_type=MESH)

    def sib_wanted(way, n, core):
        t, sub, q = split(n)
        zz = shard(way, t)
        use = jnp.logical_or(
            div(zz, SEG) == zh, jnp.logical_and(hub, div(zz, RING // 2) == core))
        return jnp.logical_and(exists(way, t, sub), use)

    def chain_place(core):
        if core == 0:
            return rem(x - zl + XS, XS), rem(x + 1, XS)
        return rem(zl - x + XS, XS), rem(x + XS - 1, XS)

    def chain_copy(core, way, m):
        t, sub, q = split(m)
        zz = shard(way, t)
        _, nxt = chain_place(core)
        to = LINE + rem(zz, RING // 2) * 2 + core
        slot = jnp.where(hub, zz * 2 + core, to)
        return pltpu.make_async_remote_copy(
            src_ref=chunk(slot, q), dst_ref=chunk(to, q),
            send_sem=chain_send.at[core, way, m], recv_sem=chain_recv.at[core, way, m],
            device_id=place(nxt, z, k), device_id_type=MESH)

    def chain_wanted(way, m):
        t, sub, q = split(m)
        mine = div(shard(way, t), RING // 2) == k
        inside = jnp.logical_and(m >= 0, m < STEPS)
        return jnp.logical_and(inside, jnp.logical_and(exists(way, t, sub), mine))

    def gather(n):
        t, sub, q = split(n)
        for way in (0, 1):
            @pl.when(jnp.logical_and(n < STEPS, t <= reach(way, sub)))
            def _():
                @pl.when(t >= 1)
                def _():
                    arrival(shard(way, t) * 2 + k, q, ring_recv.at[way, n]).wait()

                @pl.when(t < reach(way, sub))
                def _():
                    ring_copy(way, n).start()

                @pl.when(sib_wanted(way, n, 1 - k))
                def _():
                    sib_copy(way, n).start()
        m = jnp.maximum(n - LAG, 0)
        for way in (0, 1):
            @pl.when(jnp.logical_and(jnp.logical_and(n >= LAG, n < STEPS + LAG), sib_wanted(way, m, k)))
            def _():
                t, _, q = split(m)
                arrival(shard(way, t) * 2 + 1 - k, q, sib_recv.at[way, m]).wait()
        for core in (0, 1):
            far, _ = chain_place(core)
            raw = n - LAG - LAG * far
            m = jnp.maximum(raw, 0)
            for way in (0, 1):
                @pl.when(jnp.logical_and(raw >= 0, chain_wanted(way, m)))
                def _():
                    @pl.when(far >= 1)
                    def _():
                        t, _, q = split(m)
                        zz = shard(way, t)
                        slot = LINE + rem(zz, RING // 2) * 2 + core
                        arrival(slot, q, chain_recv.at[core, way, m]).wait()

                    @pl.when(far < XS - 1)
                    def _():
                        chain_copy(core, way, m).start()

    def settle(n, _):
        t, sub, q = split(n)
        for way in (0, 1):
            @pl.when(t < reach(way, sub))
            def _():
                ring_copy(way, n).wait_send()

            @pl.when(sib_wanted(way, n, 1 - k))
            def _():
                sib_copy(way, n).wait_send()

            for core in (0, 1):
                far, _ = chain_place(core)

                @pl.when(jnp.logical_and(far < XS - 1, chain_wanted(way, n)))
                def _():
                    chain_copy(core, way, n).wait_send()
        return 0

    width = vis.shape[3]
    height = vis.shape[2]
    half = width // 2
    lanes = TILE[1]
    row_base = zh * (2 * SEG)
    col_base = jnp.where(hub, k * HALF, LINE)

    def part_copy(phase, target):
        return pltpu.make_async_remote_copy(
            src_ref=sbuf.at[phase, target], dst_ref=rbuf.at[phase, r],
            send_sem=part_send.at[phase], recv_sem=part_recv.at[phase],
            device_id={"row": target, "col": c}, device_id_type=MESH)

    def hand_in(phase, target):
        @pl.when(target != r)
        def _():
            part_copy(phase, target).start()

        @pl.when(target == r)
        def _():
            rbuf[phase, r] = sbuf[phase, r]

    def put(phase, target, first, value):
        for j in range(half // lanes):
            sbuf[phase, target, first + j : first + j + 1, :] = value[:, j * lanes : (j + 1) * lanes]

    def fold(value):
        return jnp.sum(value.reshape(ROWS // 8, 8, half), axis=0)

    def wide(value):
        return jnp.concatenate([value] * (half // lanes), axis=1)

    def along(ch, rows, cols, plain):
        mr = mod[ch, 0, rows, cols].astype(F32)
        mi = mod[ch, 1, rows, cols].astype(F32)
        if plain:
            return mr, mi
        gr = wide(spread[ch, 0, rows, :])
        gi = wide(spread[ch, 1, rows, :])
        return gr * mr - gi * mi, gr * mi + gi * mr

    def normal_sums(phase, ch):
        for b in (0, 1):
            cols = slice(b * half, (b + 1) * half)

            def body(i, acc):
                rows = pl.ds(pl.multiple_of(i * ROWS, ROWS), ROWS)
                vr = vis[ch, 0, rows, cols]
                vi = vis[ch, 1, rows, cols]
                ar, ai = along(ch, rows, cols, phase == 0)
                return (
                    acc[0] + fold(vr * ar + vi * ai),
                    acc[1] + fold(vr * ai - vi * ar),
                    acc[2] + fold(ar * ar + ai * ai),
                )

            zero = jnp.zeros((8, half), F32)
            sums = lax.fori_loop(0, height // ROWS, body, (zero, zero, zero), unroll=4)
            for i, value in enumerate(sums):
                put(phase, 2 * ch + b, 2 * i, jnp.sum(value, axis=0, keepdims=True))
            hand_in(phase, 2 * ch + b)

    def misfit_sums(phase, ch):
        for b in (0, 1):
            cols = slice(b * half, (b + 1) * half)
            cr = jnp.concatenate([cbuf[2 * ch + b, 0:1, :], cbuf[2 * ch + b, 1:2, :]], axis=1)
            ci = jnp.concatenate([cbuf[2 * ch + b, 2:3, :], cbuf[2 * ch + b, 3:4, :]], axis=1)

            def body(i, acc):
                rows = pl.ds(pl.multiple_of(i * ROWS, ROWS), ROWS)
                ar, ai = along(ch, rows, cols, False)
                er = vis[ch, 0, rows, cols] - (ar * cr + ai * ci)
                ei = vis[ch, 1, rows, cols] - (ai * cr - ar * ci)
                return acc + fold(er * er + ei * ei)

            total_here = lax.fori_loop(0, height // ROWS, body, jnp.zeros((8, half), F32), unroll=4)
            put(phase, 2 * ch + b, 0, jnp.sum(total_here, axis=0, keepdims=True))
            hand_in(phase, 2 * ch + b)

    def no_diagonal(ref, ch):
        for b in (0, 1):
            @pl.when(jnp.logical_and(own_row, odd == b))
            def _():
                for comp in (0, 1):
                    def body(i, _):
                        for j in range(half // lanes):
                            rows = pl.ds(pl.multiple_of(j * lanes + i * ROWS, ROWS), ROWS)
                            cols = slice(b * half + j * lanes, b * half + (j + 1) * lanes)
                            row_id = lax.broadcasted_iota(jnp.int32, (ROWS, lanes), 0) + i * ROWS
                            col_id = lax.broadcasted_iota(jnp.int32, (ROWS, lanes), 1)
                            tile = ref[ch, comp, rows, cols].astype(F32)
                            ref[ch, comp, rows, cols] = jnp.where(row_id == col_id, 0.0, tile).astype(ref.dtype)
                        return 0

                    lax.fori_loop(0, lanes // ROWS, body, 0)

    def correlate(ch):
        row_re = buf[pl.ds(row_base, 2 * SEG), ch, 0].reshape(height, samples)
        row_im = buf[pl.ds(row_base, 2 * SEG), ch, 1].reshape(height, samples)
        col_re = buf[pl.ds(col_base, HALF), ch, 0].reshape(width, samples)
        col_im = buf[pl.ds(col_base, HALF), ch, 1].reshape(width, samples)

        left = jnp.concatenate(
            [jnp.concatenate([row_re, row_im], axis=1), jnp.concatenate([row_im, -row_re], axis=1)], axis=0)
        right = jnp.concatenate([col_re, col_im], axis=1)
        product = lax.dot_general(left, right, (((1,), (1,)), ((), ())), preferred_element_type=F32) * (1.0 / samples)
        vis[ch, 0] = product[:height]
        vis[ch, 1] = product[height:]

    def collect(phase):
        part = rbuf.at[phase, pl.ds(0, 2 * channels - 1)]
        pltpu.make_async_copy(part, part, part_recv.at[phase]).wait()
        total[...] = jnp.sum(rbuf[phase], axis=0)

    def gain_copy(phase, i):
        return pltpu.make_async_remote_copy(
            src_ref=gtile.at[phase], dst_ref=gbuf.at[phase, div(r, 2)],
            send_sem=gain_send.at[phase], recv_sem=gain_recv.at[phase, div(r, 2)],
            device_id={"row": 2 * c + odd, "col": i}, device_id_type=MESH)

    def col_copy(tile, dst, send, recv, i):
        return pltpu.make_async_remote_copy(
            src_ref=tile, dst_ref=dst.at[r], send_sem=send, recv_sem=recv,
            device_id={"row": i, "col": c}, device_id_type=MESH)

    def to_column(tile, dst, send, recv):
        def body(i, _):
            @pl.when(i != r)
            def _():
                col_copy(tile, dst, send, recv.at[own_group], i).start()
            return 0

        lax.fori_loop(0, 2 * channels, body, 0)
        dst[r] = tile[...]

    def wait_column(dst, recv, group):
        tiles = 2 * per_group
        for count, there in ((tiles - 1, own_group == group), (tiles, own_group != group)):
            @pl.when(there)
            def _():
                part = dst.at[pl.ds(0, count)]
                pltpu.make_async_copy(part, part, recv.at[group]).wait()

    def sent_column(dst, sem):
        part = dst.at[pl.ds(0, 2 * channels - 1)]
        pltpu.make_async_copy(part, part, sem).wait()

    def own_gains(phase):
        collect(phase)
        den = total[4:6, :] + EPSILON
        fresh_re = total[0:2, :] / den
        fresh_im = total[2:4, :] / den
        if phase % 2 == 1:
            fresh_re = (fresh_re + gtile[phase - 1, 0:2, :]) * 0.5
            fresh_im = (fresh_im + gtile[phase - 1, 2:4, :]) * 0.5
        gtile[phase, 0:2, :] = fresh_re
        gtile[phase, 2:4, :] = fresh_im

        def body(i, _):
            @pl.when(jnp.logical_not(jnp.logical_and(own_row, i == c)))
            def _():
                gain_copy(phase, i).start()
            return 0

        lax.fori_loop(0, channels, body, 0)

        @pl.when(own_row)
        def _():
            gbuf[phase, div(r, 2)] = gtile[phase]
        if phase == 2:
            to_column(gtile.at[2], cbuf, col_send, col_recv)

    def own_misfit():
        collect(3)
        mtile[0:2, :] = total[0:2, :] / (inputs - 1)
        to_column(mtile, mbuf, mis_send, mis_recv)

    def owners(group, task, *args):
        @pl.when(own_group == group)
        def _():
            task(*args)

    def take_gains(phase, ch):
        @pl.when(jnp.logical_not(jnp.logical_and(own_row, ch == c)))
        def _():
            part = gbuf.at[phase, ch]
            pltpu.make_async_copy(part, part, gain_recv.at[phase, ch]).wait()
        for comp in (0, 1):
            for j in range(height // lanes):
                line = gbuf[phase, ch, 2 * comp + j : 2 * comp + j + 1, :]
                spread[ch, comp, j * lanes : (j + 1) * lanes, :] = jnp.broadcast_to(line, (lanes, lanes)).T

    def each(group, task):
        def body(i, _):
            task(group * per_group + i)
            return 0

        lax.fori_loop(0, per_group, body, 0)

    def first(ch):
        correlate(ch)
        normal_sums(0, ch)

    def again(phase):
        def task(ch):
            take_gains(phase - 1, ch)
            normal_sums(phase, ch)
        return task

    def last(ch):
        take_gains(2, ch)
        misfit_sums(3, ch)

    def clear(ref):
        def body(ch, _):
            no_diagonal(ref, ch)
            return 0

        lax.fori_loop(0, channels, body, 0)

    ready = SPAN + LAG * XS

    def step(n, _):
        gather(n)
        at = jnp.maximum(n - ready, 0)
        inside = jnp.logical_and(n >= ready, n < ready + 2 * per_group)

        @pl.when(n == 4)
        def _():
            load_model.wait()
            clear(mod)

        @pl.when(jnp.logical_and(inside, rem(at, 2) == 0))
        def _():
            correlate(div(at, 2))

        @pl.when(jnp.logical_and(inside, rem(at, 2) == 1))
        def _():
            normal_sums(0, div(at, 2))
        return 0

    lax.fori_loop(0, STEPS + LAG * XS, step, 0)

    owners(0, own_gains, 0)
    each(1, first)
    each(0, again(1))
    owners(1, own_gains, 0)
    owners(0, own_gains, 1)
    each(1, again(1))
    each(0, again(2))
    owners(1, own_gains, 1)
    owners(0, own_gains, 2)
    each(1, again(2))
    clear(vis)
    wait_column(cbuf, col_recv, 0)
    each(0, last)
    owners(1, own_gains, 2)
    owners(0, own_misfit)
    wait_column(cbuf, col_recv, 1)
    each(1, last)
    lax.fori_loop(0, STEPS, settle, 0)
    for ch in range(channels):
        for b in (0, 1):
            for j in range(half // lanes):
                cols = slice(b * half + j * lanes, b * half + (j + 1) * lanes)
                for comp in (0, 1):
                    gains_out[ch, comp : comp + 1, cols] = cbuf[2 * ch + b, 2 * comp + j : 2 * comp + j + 1, :]

    owners(1, own_misfit)

    for phase in range(4):
        part = sbuf.at[phase, pl.ds(0, 2 * channels - 1)]
        pltpu.make_async_copy(part, part, part_send.at[phase]).wait()
    for phase in range(3):
        for sent, there in ((channels - 1, own_row), (channels, jnp.logical_not(own_row))):
            @pl.when(there)
            def _():
                part = gbuf.at[phase, pl.ds(0, sent)]
                pltpu.make_async_copy(part, part, gain_send.at[phase]).wait()
    sent_column(cbuf, col_send)
    sent_column(mbuf, mis_send)
    wait_column(mbuf, mis_recv, 0)
    wait_column(mbuf, mis_recv, 1)
    for ch in range(channels):
        for b in (0, 1):
            for j in range(half // lanes):
                cols = slice(b * half + j * lanes, b * half + (j + 1) * lanes)
                misfit_out[ch : ch + 1, cols] = mbuf[2 * ch + b, j : j + 1, :]


def per_device(voltages, model):
    channels, _, shard_rows, samples = voltages.shape
    height, width = model.shape[2:]
    dma = pltpu.SemaphoreType.DMA
    return pl.pallas_call(
        kernel,
        out_shape=(
            jax.ShapeDtypeStruct((channels, 2, width), F32),
            jax.ShapeDtypeStruct((channels, width), F32),
        ),
        in_specs=[pl.BlockSpec(memory_space=pl.ANY)] * 2,
        out_specs=(pl.BlockSpec(memory_space=pltpu.VMEM),) * 2,
        scratch_shapes=[
            pltpu.VMEM((LINE + HALF,) + voltages.shape, voltages.dtype),
            pltpu.VMEM(model.shape, model.dtype),
            pltpu.VMEM((channels, 2, height, width), F32),
            pltpu.VMEM((channels, 2, height, TILE[1]), F32),
            pltpu.VMEM((4, 2 * channels) + TILE, F32),
            pltpu.VMEM((4, 2 * channels) + TILE, F32),
            pltpu.VMEM(TILE, F32),
            pltpu.VMEM((3,) + TILE, F32),
            pltpu.VMEM((3, channels) + TILE, F32),
            pltpu.VMEM((2 * channels,) + TILE, F32),
            pltpu.VMEM(TILE, F32),
            pltpu.VMEM((2 * channels,) + TILE, F32),
            dma((2,)),
            dma((2, STEPS)),
            dma((2, STEPS)),
            dma((2, STEPS)),
            dma((2, STEPS)),
            dma((2, 2, STEPS)),
            dma((2, 2, STEPS)),
            dma((4,)),
            dma((4,)),
            dma((3,)),
            dma((3, channels)),
            dma(()),
            dma((2,)),
            dma(()),
            dma((2,)),
        ],
        compiler_params=pltpu.CompilerParams(
            collective_id=0, has_side_effects=True, vmem_limit_bytes=50 * 2**20
        ),
    )(voltages, model)


def solution(mesh):
    return jax.shard_map(
        per_device,
        mesh=mesh,
        in_specs=(P("chan", None, ("row", "col"), None), P("chan", None, "row", "col")),
        out_specs=(P("chan", None, "col"), P("chan", "col")),
        check_vma=False,
    )
```

```python
import functools

import jax
import jax.numpy as jnp
from jax import lax
from jax.experimental import pallas as pl
from jax.experimental.pallas import tpu as pltpu
from jax.sharding import PartitionSpec as P

EPSILON = 1e-06
MESH = pl.DeviceIdType.MESH
F32 = jnp.float32

RING = 16
SEG = 4
XS = 4
LINE = 2 * RING
HALF = RING
GROUPS = 2
SUBS = 4
STEPS = (RING // 2 + 1) * SUBS
LAG = 4
ROWS = 32
TILE = (8, 128)


def div(a, b):
    return lax.div(a, jnp.int32(b))


def rem(a, b):
    return lax.rem(a, jnp.int32(b))


def kernel(
    volts, model, gains_out, misfit_out,
    buf, mod, vis, spread, sbuf, rbuf, total, gtile, gbuf, cbuf, mtile, mbuf,
    load_sem, ring_send, ring_recv, sib_send, sib_recv, chain_send, chain_recv,
    part_send, part_recv, gain_send, gain_recv, col_send, col_recv, mis_send, mis_recv,
):
    channels = mod.shape[0]
    samples = volts.shape[3]
    per_chunk = channels // SUBS
    per_group = channels // GROUPS
    inputs = 4096
    r = lax.axis_index("row")
    c = lax.axis_index("col")
    x, zh = div(r, SEG), rem(r, SEG)
    zl, k = div(c, 2), rem(c, 2)
    z = zh * SEG + zl
    hub = x == zl
    odd = rem(r, 2)
    own_group = div(r, 2 * per_group)
    own_row = div(r, 2) == c

    def place(xx, zz, kk):
        return {"row": xx * SEG + div(zz, SEG), "col": rem(zz, SEG) * 2 + kk}

    own_slot = z * 2 + k
    load_volts = pltpu.make_async_copy(volts, buf.at[own_slot], load_sem.at[0])
    load_model = pltpu.make_async_copy(model, mod, load_sem.at[1])
    load_volts.start()
    load_model.start()

    barrier = pltpu.get_barrier_semaphore()

    def signal(target):
        pl.semaphore_signal(barrier, inc=1, device_id=target, device_id_type=MESH)

    signal(place(x, rem(z + 1, RING), k))
    signal(place(x, rem(z + RING - 1, RING), k))
    signal(place(x, z, 1 - k))

    def greet(i, _):
        @pl.when(i != r)
        def _():
            signal({"row": i, "col": c})
        return 0

    lax.fori_loop(0, 2 * channels, greet, 0)

    def greet_owner(ch, _):
        @pl.when(jnp.logical_not(jnp.logical_and(own_row, ch == c)))
        def _():
            signal({"row": 2 * ch + odd, "col": div(r, 2)})
        return 0

    lax.fori_loop(0, channels, greet_owner, 0)
    sbuf[...] = jnp.zeros(sbuf.shape, F32)
    gtile[...] = jnp.zeros(gtile.shape, F32)
    mtile[...] = jnp.zeros(mtile.shape, F32)
    load_volts.wait()
    pl.semaphore_wait(barrier, 3 + 2 * channels - 1 + channels - own_row.astype(jnp.int32))

    def split(n):
        sub = rem(n, SUBS)
        return div(n, SUBS), sub, sub

    def chunk(slot, q):
        return buf.at[slot, pl.ds(q * per_chunk, per_chunk)]

    def reach(way, sub):
        return RING // 2 - rem(sub + way, 2)

    def shard(way, t):
        return rem(z - t + RING, RING) if way == 0 else rem(z + t, RING)

    def exists(way, t, sub):
        here = t <= reach(way, sub)
        return here if way == 0 else jnp.logical_and(here, t >= 1)

    def ring_copy(way, n):
        t, sub, q = split(n)
        slot = shard(way, t) * 2 + k
        nxt = rem(z + 1, RING) if way == 0 else rem(z + RING - 1, RING)
        return pltpu.make_async_remote_copy(
            src_ref=chunk(slot, q), dst_ref=chunk(slot, q),
            send_sem=ring_send.at[way, n], recv_sem=ring_recv.at[way, n + SUBS],
            device_id=place(x, nxt, k), device_id_type=MESH)

    def arrival(slot, q, sem):
        return pltpu.make_async_copy(chunk(slot, q), chunk(slot, q), sem)

    def sib_copy(way, n):
        t, sub, q = split(n)
        slot = shard(way, t) * 2 + k
        return pltpu.make_async_remote_copy(
            src_ref=chunk(slot, q), dst_ref=chunk(slot, q),
            send_sem=sib_send.at[way, n], recv_sem=sib_recv.at[way, n],
            device_id=place(x, z, 1 - k), device_id_type=MESH)

    def sib_wanted(way, n, core):
        t, sub, q = split(n)
        zz = shard(way, t)
        use = jnp.logical_or(
            div(zz, SEG) == zh, jnp.logical_and(hub, div(zz, RING // 2) == core))
        return jnp.logical_and(exists(way, t, sub), use)

    def chain_place(core):
        if core == 0:
            return rem(x - zl + XS, XS), rem(x + 1, XS)
        return rem(zl - x + XS, XS), rem(x + XS - 1, XS)

    def chain_copy(core, way, m):
        t, sub, q = split(m)
        zz = shard(way, t)
        _, nxt = chain_place(core)
        to = LINE + rem(zz, RING // 2) * 2 + core
        slot = jnp.where(hub, zz * 2 + core, to)
        return pltpu.make_async_remote_copy(
            src_ref=chunk(slot, q), dst_ref=chunk(to, q),
            send_sem=chain_send.at[core, way, m], recv_sem=chain_recv.at[core, way, m],
            device_id=place(nxt, z, k), device_id_type=MESH)

    def chain_wanted(way, m):
        t, sub, q = split(m)
        mine = div(shard(way, t), RING // 2) == k
        inside = jnp.logical_and(m >= 0, m < STEPS)
        return jnp.logical_and(inside, jnp.logical_and(exists(way, t, sub), mine))

    def gather(n):
        t, sub, q = split(n)
        for way in (0, 1):
            @pl.when(jnp.logical_and(n < STEPS, t <= reach(way, sub)))
            def _():
                @pl.when(t >= 1)
                def _():
                    arrival(shard(way, t) * 2 + k, q, ring_recv.at[way, n]).wait()

                @pl.when(t < reach(way, sub))
                def _():
                    ring_copy(way, n).start()

                @pl.when(sib_wanted(way, n, 1 - k))
                def _():
                    sib_copy(way, n).start()
        m = jnp.maximum(n - LAG, 0)
        for way in (0, 1):
            @pl.when(jnp.logical_and(jnp.logical_and(n >= LAG, n < STEPS + LAG), sib_wanted(way, m, k)))
            def _():
                t, _, q = split(m)
                arrival(shard(way, t) * 2 + 1 - k, q, sib_recv.at[way, m]).wait()
        for core in (0, 1):
            far, _ = chain_place(core)
            raw = n - LAG - LAG * far
            m = jnp.maximum(raw, 0)
            for way in (0, 1):
                @pl.when(jnp.logical_and(raw >= 0, chain_wanted(way, m)))
                def _():
                    @pl.when(far >= 1)
                    def _():
                        t, _, q = split(m)
                        zz = shard(way, t)
                        slot = LINE + rem(zz, RING // 2) * 2 + core
                        arrival(slot, q, chain_recv.at[core, way, m]).wait()

                    @pl.when(far < XS - 1)
                    def _():
                        chain_copy(core, way, m).start()

    def settle(n, _):
        t, sub, q = split(n)
        for way in (0, 1):
            @pl.when(t < reach(way, sub))
            def _():
                ring_copy(way, n).wait_send()

            @pl.when(sib_wanted(way, n, 1 - k))
            def _():
                sib_copy(way, n).wait_send()

            for core in (0, 1):
                far, _ = chain_place(core)

                @pl.when(jnp.logical_and(far < XS - 1, chain_wanted(way, n)))
                def _():
                    chain_copy(core, way, n).wait_send()
        return 0

    width = vis.shape[3]
    height = vis.shape[2]
    half = width // 2
    lanes = TILE[1]
    row_base = zh * (2 * SEG)
    col_base = jnp.where(hub, k * HALF, LINE)

    def part_copy(phase, target):
        return pltpu.make_async_remote_copy(
            src_ref=sbuf.at[phase, target], dst_ref=rbuf.at[phase, r],
            send_sem=part_send.at[phase], recv_sem=part_recv.at[phase],
            device_id={"row": target, "col": c}, device_id_type=MESH)

    def hand_in(phase, target):
        @pl.when(target != r)
        def _():
            part_copy(phase, target).start()

        @pl.when(target == r)
        def _():
            rbuf[phase, r] = sbuf[phase, r]

    def put(phase, target, first, value):
        for j in range(half // lanes):
            sbuf[phase, target, first + j : first + j + 1, :] = value[:, j * lanes : (j + 1) * lanes]

    def fold(value):
        return jnp.sum(value.reshape(ROWS // 8, 8, half), axis=0)

    def wide(value):
        return jnp.concatenate([value] * (half // lanes), axis=1)

    def along(ch, rows, cols, plain):
        mr = mod[ch, 0, rows, cols].astype(F32)
        mi = mod[ch, 1, rows, cols].astype(F32)
        if plain:
            return mr, mi
        gr = wide(spread[ch, 0, rows, :])
        gi = wide(spread[ch, 1, rows, :])
        return gr * mr - gi * mi, gr * mi + gi * mr

    def normal_sums(phase, ch):
        for b in (0, 1):
            cols = slice(b * half, (b + 1) * half)

            def body(i, acc):
                rows = pl.ds(pl.multiple_of(i * ROWS, ROWS), ROWS)
                vr = vis[ch, 0, rows, cols]
                vi = vis[ch, 1, rows, cols]
                ar, ai = along(ch, rows, cols, phase == 0)
                return (
                    acc[0] + fold(vr * ar + vi * ai),
                    acc[1] + fold(vr * ai - vi * ar),
                    acc[2] + fold(ar * ar + ai * ai),
                )

            zero = jnp.zeros((8, half), F32)
            sums = lax.fori_loop(0, height // ROWS, body, (zero, zero, zero), unroll=2)
            for i, value in enumerate(sums):
                put(phase, 2 * ch + b, 2 * i, jnp.sum(value, axis=0, keepdims=True))
            hand_in(phase, 2 * ch + b)

    def misfit_sums(phase, ch):
        for b in (0, 1):
            cols = slice(b * half, (b + 1) * half)
            cr = jnp.concatenate([cbuf[2 * ch + b, 0:1, :], cbuf[2 * ch + b, 1:2, :]], axis=1)
            ci = jnp.concatenate([cbuf[2 * ch + b, 2:3, :], cbuf[2 * ch + b, 3:4, :]], axis=1)

            def body(i, acc):
                rows = pl.ds(pl.multiple_of(i * ROWS, ROWS), ROWS)
                ar, ai = along(ch, rows, cols, False)
                er = vis[ch, 0, rows, cols] - (ar * cr + ai * ci)
                ei = vis[ch, 1, rows, cols] - (ai * cr - ar * ci)
                return acc + fold(er * er + ei * ei)

            total_here = lax.fori_loop(0, height // ROWS, body, jnp.zeros((8, half), F32), unroll=2)
            put(phase, 2 * ch + b, 0, jnp.sum(total_here, axis=0, keepdims=True))
            hand_in(phase, 2 * ch + b)

    def no_diagonal(ref, ch):
        for b in (0, 1):
            @pl.when(jnp.logical_and(own_row, odd == b))
            def _():
                for comp in (0, 1):
                    def body(i, _):
                        for j in range(half // lanes):
                            rows = pl.ds(pl.multiple_of(j * lanes + i * ROWS, ROWS), ROWS)
                            cols = slice(b * half + j * lanes, b * half + (j + 1) * lanes)
                            row_id = lax.broadcasted_iota(jnp.int32, (ROWS, lanes), 0) + i * ROWS
                            col_id = lax.broadcasted_iota(jnp.int32, (ROWS, lanes), 1)
                            tile = ref[ch, comp, rows, cols].astype(F32)
                            ref[ch, comp, rows, cols] = jnp.where(row_id == col_id, 0.0, tile).astype(ref.dtype)
                        return 0

                    lax.fori_loop(0, lanes // ROWS, body, 0)

    def correlate(ch):
        row_re = buf[pl.ds(row_base, 2 * SEG), ch, 0].reshape(height, samples)
        row_im = buf[pl.ds(row_base, 2 * SEG), ch, 1].reshape(height, samples)
        col_re = buf[pl.ds(col_base, HALF), ch, 0].reshape(width, samples)
        col_im = buf[pl.ds(col_base, HALF), ch, 1].reshape(width, samples)

        left = jnp.concatenate(
            [jnp.concatenate([row_re, row_im], axis=1), jnp.concatenate([row_im, -row_re], axis=1)], axis=0)
        right = jnp.concatenate([col_re, col_im], axis=1)
        product = lax.dot_general(left, right, (((1,), (1,)), ((), ())), preferred_element_type=F32) * (1.0 / samples)
        vis[ch, 0] = product[:height]
        vis[ch, 1] = product[height:]

    def collect(phase):
        part = rbuf.at[phase, pl.ds(0, 2 * channels - 1)]
        pltpu.make_async_copy(part, part, part_recv.at[phase]).wait()
        total[...] = jnp.sum(rbuf[phase], axis=0)

    def gain_copy(phase, i):
        return pltpu.make_async_remote_copy(
            src_ref=gtile.at[phase], dst_ref=gbuf.at[phase, div(r, 2)],
            send_sem=gain_send.at[phase], recv_sem=gain_recv.at[phase, div(r, 2)],
            device_id={"row": 2 * c + odd, "col": i}, device_id_type=MESH)

    def col_copy(tile, dst, send, recv, i):
        return pltpu.make_async_remote_copy(
            src_ref=tile, dst_ref=dst.at[r], send_sem=send, recv_sem=recv,
            device_id={"row": i, "col": c}, device_id_type=MESH)

    def to_column(tile, dst, send, recv):
        def body(i, _):
            @pl.when(i != r)
            def _():
                col_copy(tile, dst, send, recv.at[own_group], i).start()
            return 0

        lax.fori_loop(0, 2 * channels, body, 0)
        dst[r] = tile[...]

    def wait_column(dst, recv, group):
        tiles = 2 * per_group
        for count, there in ((tiles - 1, own_group == group), (tiles, own_group != group)):
            @pl.when(there)
            def _():
                part = dst.at[pl.ds(0, count)]
                pltpu.make_async_copy(part, part, recv.at[group]).wait()

    def sent_column(dst, sem):
        part = dst.at[pl.ds(0, 2 * channels - 1)]
        pltpu.make_async_copy(part, part, sem).wait()

    def own_gains(phase):
        collect(phase)
        den = total[4:6, :] + EPSILON
        fresh_re = total[0:2, :] / den
        fresh_im = total[2:4, :] / den
        if phase % 2 == 1:
            fresh_re = (fresh_re + gtile[phase - 1, 0:2, :]) * 0.5
            fresh_im = (fresh_im + gtile[phase - 1, 2:4, :]) * 0.5
        gtile[phase, 0:2, :] = fresh_re
        gtile[phase, 2:4, :] = fresh_im

        def body(i, _):
            @pl.when(jnp.logical_not(jnp.logical_and(own_row, i == c)))
            def _():
                gain_copy(phase, i).start()
            return 0

        lax.fori_loop(0, channels, body, 0)

        @pl.when(own_row)
        def _():
            gbuf[phase, div(r, 2)] = gtile[phase]
        if phase == 2:
            to_column(gtile.at[2], cbuf, col_send, col_recv)

    def own_misfit():
        collect(3)
        mtile[0:2, :] = total[0:2, :] / (inputs - 1)
        to_column(mtile, mbuf, mis_send, mis_recv)

    def owners(group, task, *args):
        @pl.when(own_group == group)
        def _():
            task(*args)

    def take_gains(phase, ch):
        @pl.when(jnp.logical_not(jnp.logical_and(own_row, ch == c)))
        def _():
            part = gbuf.at[phase, ch]
            pltpu.make_async_copy(part, part, gain_recv.at[phase, ch]).wait()
        for comp in (0, 1):
            for j in range(height // lanes):
                line = gbuf[phase, ch, 2 * comp + j : 2 * comp + j + 1, :]
                spread[ch, comp, j * lanes : (j + 1) * lanes, :] = jnp.broadcast_to(line, (lanes, lanes)).T

    def each(group, task):
        def body(i, _):
            task(group * per_group + i)
            return 0

        lax.fori_loop(0, per_group, body, 0)

    def first(ch):
        correlate(ch)
        normal_sums(0, ch)

    def again(phase):
        def task(ch):
            take_gains(phase - 1, ch)
            normal_sums(phase, ch)
        return task

    def last(ch):
        take_gains(2, ch)
        misfit_sums(3, ch)

    def clear(ref):
        def body(ch, _):
            no_diagonal(ref, ch)
            return 0

        lax.fori_loop(0, channels, body, 0)

    def step(n, _):
        gather(n)

        @pl.when(n == SUBS - 1)
        def _():
            load_model.wait()
            clear(mod)
        return 0

    lax.fori_loop(0, STEPS + LAG * XS, step, 0)

    third = STEPS // 3
    each(0, first)
    each(1, first)
    for phase in (0, 1, 2):
        owners(0, own_gains, phase)
        owners(1, own_gains, phase)
        lax.fori_loop(phase * third, (phase + 1) * third, settle, 0)
        if phase < 2:
            each(0, again(phase + 1))
            each(1, again(phase + 1))
    clear(vis)
    wait_column(cbuf, col_recv, 0)
    each(0, last)
    wait_column(cbuf, col_recv, 1)
    each(1, last)
    owners(0, own_misfit)
    owners(1, own_misfit)
    for ch in range(channels):
        for b in (0, 1):
            for j in range(half // lanes):
                cols = slice(b * half + j * lanes, b * half + (j + 1) * lanes)
                for comp in (0, 1):
                    gains_out[ch, comp : comp + 1, cols] = cbuf[2 * ch + b, 2 * comp + j : 2 * comp + j + 1, :]


    for phase in range(4):
        part = sbuf.at[phase, pl.ds(0, 2 * channels - 1)]
        pltpu.make_async_copy(part, part, part_send.at[phase]).wait()
    for phase in range(3):
        for sent, there in ((channels - 1, own_row), (channels, jnp.logical_not(own_row))):
            @pl.when(there)
            def _():
                part = gbuf.at[phase, pl.ds(0, sent)]
                pltpu.make_async_copy(part, part, gain_send.at[phase]).wait()
    sent_column(cbuf, col_send)
    sent_column(mbuf, mis_send)
    wait_column(mbuf, mis_recv, 0)
    wait_column(mbuf, mis_recv, 1)
    for ch in range(channels):
        for b in (0, 1):
            for j in range(half // lanes):
                cols = slice(b * half + j * lanes, b * half + (j + 1) * lanes)
                misfit_out[ch : ch + 1, cols] = mbuf[2 * ch + b, j : j + 1, :]


def per_device(voltages, model):
    channels, _, shard_rows, samples = voltages.shape
    height, width = model.shape[2:]
    dma = pltpu.SemaphoreType.DMA
    return pl.pallas_call(
        kernel,
        out_shape=(
            jax.ShapeDtypeStruct((channels, 2, width), F32),
            jax.ShapeDtypeStruct((channels, width), F32),
        ),
        in_specs=[pl.BlockSpec(memory_space=pl.ANY)] * 2,
        out_specs=(pl.BlockSpec(memory_space=pltpu.VMEM),) * 2,
        scratch_shapes=[
            pltpu.VMEM((LINE + HALF,) + voltages.shape, voltages.dtype),
            pltpu.VMEM(model.shape, model.dtype),
            pltpu.VMEM((channels, 2, height, width), F32),
            pltpu.VMEM((channels, 2, height, TILE[1]), F32),
            pltpu.VMEM((4, 2 * channels) + TILE, F32),
            pltpu.VMEM((4, 2 * channels) + TILE, F32),
            pltpu.VMEM(TILE, F32),
            pltpu.VMEM((3,) + TILE, F32),
            pltpu.VMEM((3, channels) + TILE, F32),
            pltpu.VMEM((2 * channels,) + TILE, F32),
            pltpu.VMEM(TILE, F32),
            pltpu.VMEM((2 * channels,) + TILE, F32),
            dma((2,)),
            dma((2, STEPS)),
            dma((2, STEPS)),
            dma((2, STEPS)),
            dma((2, STEPS)),
            dma((2, 2, STEPS)),
            dma((2, 2, STEPS)),
            dma((4,)),
            dma((4,)),
            dma((3,)),
            dma((3, channels)),
            dma(()),
            dma((2,)),
            dma(()),
            dma((2,)),
        ],
        compiler_params=pltpu.CompilerParams(
            collective_id=0, has_side_effects=True, vmem_limit_bytes=50 * 2**20
        ),
    )(voltages, model)


def solution(mesh):
    return jax.shard_map(
        per_device,
        mesh=mesh,
        in_specs=(P("chan", None, ("row", "col"), None), P("chan", None, "row", "col")),
        out_specs=(P("chan", None, "col"), P("chan", "col")),
        check_vma=False,
    )
```
